32 devices in a mesh: seq: 8 (over z, y), ch: 4 (over x, core).
Axes of the slice: x: 2, y: 2, z: 4, core: 2. Of those that a mesh axis runs over, the one named last changes fastest.
Arguments:
- tokens: bfloat16 [1024, 2048], P('seq'), may hold values from -6 to 6
- in_weight: bfloat16 [2048, 3, 2048], P('seq', None, 'ch'), may hold values from -0.125 to 0.125
- filter_taps: float32 [1024, 2048], P('seq', 'ch'), may hold values from -1.1 to 1.1
- skip_gain: float32 [2048], P('ch'), may hold values from 0.5 to 1.5
- out_weight: bfloat16 [2048, 2048], P(None, 'ch'), may hold values from -0.125 to 0.125
Outputs:
- mixed: bfloat16 [1024, 2048], P('seq', 'ch')
The draws below stay inside these ranges and needn't reach their ends.
All inputs are finite; a program needn't handle non-finite values.
Results may differ from the reference program's by a relative error of at most 0.0072.
Values may be sent and summed in bfloat16 or wider, within the bound.
A program may use at most 64 MiB of HBM per device.

```python
import math
import jax
import jax.numpy as jnp
from jax import lax

D = 2048
C = 2048
TOKENS = 1024


def draw_filter_taps(key, part):
    key = jax.random.fold_in(key, 7)
    key_tau = jax.random.fold_in(key, 0)
    key_rough = jax.random.fold_in(key, 2)
    length = TOKENS
    position = jnp.arange(length, dtype=jnp.float32)[:, None]
    unit = jax.random.uniform(key_tau, (C,), dtype=jnp.float32)
    tau = jnp.exp(math.log(30.0) + unit * (math.log(2.0 * length) - math.log(30.0)))
    rough = jnp.clip(jax.random.normal(key_rough, (length, C), dtype=jnp.float32), -4.0, 4.0)
    scale = jnp.sqrt(2.0 / jnp.minimum(tau, float(length)))
    return rough * jnp.exp(-position / tau[None, :]) * scale[None, :]


def block_scale(key, dims, pieces, smallest, largest):
    level, own = 1.0, jax.random.fold_in(key, 6)
    for dim, parts in pieces:
        draws = jnp.exp(jax.random.uniform(jax.random.fold_in(own, dim), (parts,), jnp.float32, smallest / len(pieces), largest / len(pieces)))
        level = level * jnp.repeat(draws, dims[dim] // parts).reshape([-1 if axis == dim else 1 for axis in range(len(dims))])
    return level


def centred(rng, extent, scale, most, cuts=(), kind=jnp.bfloat16):
    result = jax.random.normal(rng, extent, jnp.float32) * scale
    if len(cuts) > 0:
        result = block_scale(rng, extent, cuts, -0.22, 0.18) * result
    return jnp.clip(result, min=-most, max=most).astype(kind)


def setup_inputs(seed: int = 0) -> dict:
    arg_keys = jax.random.split(jax.random.key(seed), 6)
    tokens = centred(arg_keys[0], (TOKENS, D), 1.0, 6.0, ((0, 8),))
    in_weight = centred(arg_keys[1], (D, 3, C), D ** -0.5, 0.125, ((0, 8), (2, 4)))
    filter_taps = draw_filter_taps(jax.random.fold_in(arg_keys[5], 71), 0)
    skip_gain = jnp.clip(0.5 + 1.0 * jax.random.uniform(arg_keys[3], (C,), jnp.float32) ** block_scale(arg_keys[3], (C,), ((0, 4),), -0.2, 0.2), 0.5, 1.5)
    out_weight = centred(arg_keys[4], (C, D), C ** -0.5, 0.125, ((1, 4),))
    return {"tokens": tokens, "in_weight": in_weight, "filter_taps": filter_taps, "skip_gain": skip_gain, "out_weight": out_weight}


def causal_conv(pair):
    signal_block, filter_block = pair
    total = signal_block.shape[0]
    spec_sig = jnp.fft.rfft(signal_block, n=2 * total, axis=0)
    spec_filt = jnp.fft.rfft(filter_block, n=2 * total, axis=0)
    return jnp.fft.irfft(spec_sig * spec_filt, n=2 * total, axis=0)[:total]


def reference(tokens, in_weight, filter_taps, skip_gain, out_weight):
    total = tokens.shape[0]
    channels = filter_taps.shape[1]
    projected = jnp.dot(tokens, in_weight.reshape(in_weight.shape[0], 3 * channels), preferred_element_type=jnp.float32)
    projected = projected.astype(jnp.bfloat16).reshape(total, 3, channels)
    values = projected[:, 0].astype(jnp.float32)
    in_gate = projected[:, 1].astype(jnp.float32)
    out_gate = projected[:, 2].astype(jnp.float32)
    signal = in_gate * values
    group = min(64, channels)
    count = channels // group
    sig_blocks = signal.reshape(total, count, group).transpose(1, 0, 2)
    filt_blocks = filter_taps.reshape(total, count, group).transpose(1, 0, 2)
    conv = lax.map(causal_conv, (sig_blocks, filt_blocks))
    conv = conv.transpose(1, 0, 2).reshape(total, channels)
    gated = (out_gate * (conv + skip_gain[None, :] * signal)).astype(jnp.bfloat16)
    return jnp.dot(gated, out_weight, preferred_element_type=jnp.float32).astype(jnp.bfloat16)
```

```python
import math

import jax
import jax.numpy as jnp
import numpy as np
from jax import lax
from jax.sharding import PartitionSpec as P

HIGHEST_PREC = lax.Precision.HIGHEST


def angle_table(first_index, second_index, period):
    product = first_index[:, None] * second_index[None, :] % period
    angle = 2.0 * math.pi / period * product.astype(jnp.float32)
    return (jnp.cos(angle), jnp.sin(angle))


def contract(matrix, blocks):
    return jnp.einsum("kn,...nc->...kc", matrix, blocks, precision=HIGHEST_PREC)


def rotate(real_part, imag_part, cosine, sine, direction):
    return (
        real_part * cosine - direction * imag_part * sine,
        imag_part * cosine + direction * real_part * sine,
    )


def spectral(parts):
    sig_re, sig_im, filt_re, filt_im = parts
    row_count = sig_re.shape[-2]
    index = jnp.arange(row_count, dtype=jnp.int32)
    cosine, sine = angle_table(index, index, row_count)

    def forward(real_part, imag_part):
        return (
            contract(cosine, real_part) + contract(sine, imag_part),
            contract(cosine, imag_part) - contract(sine, real_part),
        )

    spec_re, spec_im = forward(sig_re, sig_im)
    resp_re, resp_im = forward(filt_re, filt_im)
    prod_re = spec_re * resp_re - spec_im * resp_im
    prod_im = spec_re * resp_im + spec_im * resp_re
    return (
        contract(cosine, prod_re) - contract(sine, prod_im),
        contract(cosine, prod_im) + contract(sine, prod_re),
    )


def per_device_long(tokens, in_weight, filter_taps, skip_gain, out_weight):
    row_count, channel_count = filter_taps.shape
    seq_size = lax.axis_size("seq")
    seq_index = lax.axis_index("seq")
    full_len = 2 * seq_size * row_count
    radix = 2 * seq_size
    positions = jnp.arange(row_count, dtype=jnp.int32)
    piece = lax.all_gather(in_weight, "seq", axis=0, tiled=True)
    width_rows = piece.shape[0]
    projected = jnp.dot(
        tokens, piece.reshape(width_rows, 3 * channel_count), preferred_element_type=jnp.float32
    )
    projected = projected.astype(jnp.bfloat16).reshape(row_count, 3, channel_count)
    values = projected[:, 0].astype(jnp.float32)
    in_gate = projected[:, 1].astype(jnp.float32)
    out_gate = projected[:, 2].astype(jnp.float32)
    signal = in_gate * values
    block_rows = row_count // seq_size
    sig_cols, filt_cols = (
        lax.all_to_all(
            signal.reshape(1, row_count, channel_count),
            "seq",
            split_axis=1,
            concat_axis=0,
            tiled=True,
        ),
        lax.all_to_all(
            filter_taps.reshape(1, row_count, channel_count),
            "seq",
            split_axis=1,
            concat_axis=0,
            tiled=True,
        ),
    )
    first_cos, first_sin = angle_table(
        jnp.arange(radix, dtype=jnp.int32), jnp.arange(seq_size, dtype=jnp.int32), radix
    )
    offsets = seq_index * block_rows + jnp.arange(block_rows, dtype=jnp.int32)
    turn_cos, turn_sin = angle_table(jnp.arange(radix, dtype=jnp.int32), offsets, full_len)
    sectioned = []
    for column_data in (sig_cols, filt_cols):
        part_re = jnp.einsum("kp,pqc->kqc", first_cos, column_data, precision=HIGHEST_PREC)
        part_im = -jnp.einsum("kp,pqc->kqc", first_sin, column_data, precision=HIGHEST_PREC)
        turned_re, turned_im = rotate(
            part_re, part_im, turn_cos[:, :, None], turn_sin[:, :, None], -1.0
        )
        sectioned.append(turned_re.reshape(seq_size, 2, block_rows, channel_count))
        sectioned.append(turned_im.reshape(seq_size, 2, block_rows, channel_count))
    back_re, back_im = spectral(
        (
            lax.all_to_all(sectioned[0], "seq", split_axis=0, concat_axis=2, tiled=True),
            lax.all_to_all(sectioned[1], "seq", split_axis=0, concat_axis=2, tiled=True),
            lax.all_to_all(sectioned[2], "seq", split_axis=0, concat_axis=2, tiled=True),
            lax.all_to_all(sectioned[3], "seq", split_axis=0, concat_axis=2, tiled=True),
        )
    )
    own_freq = 2 * seq_index + jnp.arange(2, dtype=jnp.int32)
    inv_cos, inv_sin = angle_table(own_freq, positions, full_len)
    inner_re, inner_im = rotate(
        back_re[0], back_im[0], inv_cos[:, :, None], inv_sin[:, :, None], 1.0
    )
    gathered_re, gathered_im = (
        lax.all_to_all(inner_re, "seq", split_axis=1, concat_axis=0, tiled=True),
        lax.all_to_all(inner_im, "seq", split_axis=1, concat_axis=0, tiled=True),
    )
    last_cos, last_sin = angle_table(
        jnp.arange(seq_size, dtype=jnp.int32), jnp.arange(radix, dtype=jnp.int32), radix
    )
    rows_part = (
        jnp.einsum("pk,kqc->pqc", last_cos, gathered_re, precision=HIGHEST_PREC)
        - jnp.einsum("pk,kqc->pqc", last_sin, gathered_im, precision=HIGHEST_PREC)
    ) / full_len
    conv = lax.all_to_all(rows_part, "seq", split_axis=0, concat_axis=1, tiled=True).reshape(
        row_count, channel_count
    )
    gated = (out_gate * (conv + skip_gain[None, :] * signal)).astype(jnp.bfloat16)
    whole = lax.all_gather(gated, "ch", axis=1, tiled=True)
    return jnp.dot(whole, out_weight, preferred_element_type=jnp.float32).astype(jnp.bfloat16)


DENSE_LIMIT = 2048


def half_step_tables(total):
    index = np.arange(total, dtype=np.int64)
    product = (2 * index[:, None] + 1) * index[None, :] % (4 * total)
    angle = 2.0 * np.pi / (4 * total) * product
    return np.cos(angle), np.sin(angle)


def dot32(left, right):
    return jnp.dot(left.astype(jnp.bfloat16), right.astype(jnp.bfloat16), preferred_element_type=jnp.float32)


def per_device(tokens, in_weight, filter_taps, skip_gain, out_weight):
    row_count, channel_count = filter_taps.shape
    seq_size = lax.axis_size("seq")
    seq_index = lax.axis_index("seq")
    own = channel_count // seq_size
    total = row_count * seq_size
    cos_table, sin_table = half_step_tables(total)
    table = jnp.asarray(np.concatenate([cos_table, sin_table]), jnp.bfloat16)
    back = jnp.asarray(np.concatenate([cos_table.T, -sin_table.T], axis=1) / total, jnp.bfloat16)
    all_tokens = lax.all_gather(tokens, "seq", axis=0, tiled=True)
    weight = lax.all_to_all(
        in_weight.reshape(-1, 3, seq_size, own).transpose(2, 0, 1, 3).reshape(seq_size, -1, 128),
        "seq", split_axis=0, concat_axis=0, tiled=True,
    ).reshape(all_tokens.shape[1], 3 * own)
    taps = lax.all_to_all(
        filter_taps.astype(jnp.bfloat16).reshape(row_count, seq_size, own).transpose(1, 0, 2).reshape(seq_size, -1, 128),
        "seq", split_axis=0, concat_axis=0, tiled=True,
    ).reshape(total, own)
    gain = lax.dynamic_slice_in_dim(skip_gain, seq_index * own, own)
    projected = jnp.dot(all_tokens, weight, preferred_element_type=jnp.float32).astype(jnp.bfloat16)
    values, in_gate, out_gate = (
        projected[:, j * own : (j + 1) * own].astype(jnp.float32) for j in range(3)
    )
    signal = in_gate * values
    spec = dot32(table, signal)
    resp = dot32(table, taps)
    spec_re, spec_im, resp_re, resp_im = spec[:total], spec[total:], resp[:total], resp[total:]
    prod = jnp.concatenate(
        [spec_re * resp_re - spec_im * resp_im, -(spec_re * resp_im + spec_im * resp_re)]
    )
    conv = dot32(back, prod)
    gated = (out_gate * (conv + gain[None, :] * signal)).astype(jnp.bfloat16)
    mine = lax.all_to_all(gated.reshape(seq_size, row_count * own // 128, 128), "seq", split_axis=0, concat_axis=0, tiled=True)
    whole = lax.all_gather(mine, "ch", axis=0, tiled=True)
    whole = whole.reshape(-1, row_count, own).transpose(1, 0, 2).reshape(row_count, -1)
    return jnp.dot(whole, out_weight, preferred_element_type=jnp.float32).astype(jnp.bfloat16)


def solution(mesh):
    in_specs = (P("seq", None), P("seq", None, "ch"), P("seq", "ch"), P("ch"), P(None, "ch"))
    out_specs = P("seq", "ch")

    def whole(tokens, in_weight, filter_taps, skip_gain, out_weight):
        dense = tokens.shape[0] <= DENSE_LIMIT
        body = per_device if dense else per_device_long
        return jax.shard_map(
            body, mesh=mesh, in_specs=in_specs, out_specs=out_specs, check_vma=False
        )(tokens, in_weight, filter_taps, skip_gain, out_weight)

    return whole
```

```python
import math

import jax
import jax.numpy as jnp
import numpy as np
from jax import lax
from jax.experimental import pallas as pl
from jax.experimental.pallas import tpu as pltpu
from jax.sharding import PartitionSpec as P

HIGHEST_PREC = lax.Precision.HIGHEST


def angle_table(first_index, second_index, period):
    product = first_index[:, None] * second_index[None, :] % period
    angle = 2.0 * math.pi / period * product.astype(jnp.float32)
    return (jnp.cos(angle), jnp.sin(angle))


def contract(matrix, blocks):
    return jnp.einsum("kn,...nc->...kc", matrix, blocks, precision=HIGHEST_PREC)


def rotate(real_part, imag_part, cosine, sine, direction):
    return (
        real_part * cosine - direction * imag_part * sine,
        imag_part * cosine + direction * real_part * sine,
    )


def spectral(parts):
    sig_re, sig_im, filt_re, filt_im = parts
    row_count = sig_re.shape[-2]
    index = jnp.arange(row_count, dtype=jnp.int32)
    cosine, sine = angle_table(index, index, row_count)

    def forward(real_part, imag_part):
        return (
            contract(cosine, real_part) + contract(sine, imag_part),
            contract(cosine, imag_part) - contract(sine, real_part),
        )

    spec_re, spec_im = forward(sig_re, sig_im)
    resp_re, resp_im = forward(filt_re, filt_im)
    prod_re = spec_re * resp_re - spec_im * resp_im
    prod_im = spec_re * resp_im + spec_im * resp_re
    return (
        contract(cosine, prod_re) - contract(sine, prod_im),
        contract(cosine, prod_im) + contract(sine, prod_re),
    )


def per_device_long(tokens, in_weight, filter_taps, skip_gain, out_weight):
    row_count, channel_count = filter_taps.shape
    seq_size = lax.axis_size("seq")
    seq_index = lax.axis_index("seq")
    full_len = 2 * seq_size * row_count
    radix = 2 * seq_size
    positions = jnp.arange(row_count, dtype=jnp.int32)
    piece = lax.all_gather(in_weight, "seq", axis=0, tiled=True)
    width_rows = piece.shape[0]
    projected = jnp.dot(
        tokens, piece.reshape(width_rows, 3 * channel_count), preferred_element_type=jnp.float32
    )
    projected = projected.astype(jnp.bfloat16).reshape(row_count, 3, channel_count)
    values = projected[:, 0].astype(jnp.float32)
    in_gate = projected[:, 1].astype(jnp.float32)
    out_gate = projected[:, 2].astype(jnp.float32)
    signal = in_gate * values
    block_rows = row_count // seq_size
    sig_cols, filt_cols = (
        lax.all_to_all(
            signal.reshape(1, row_count, channel_count),
            "seq",
            split_axis=1,
            concat_axis=0,
            tiled=True,
        ),
        lax.all_to_all(
            filter_taps.reshape(1, row_count, channel_count),
            "seq",
            split_axis=1,
            concat_axis=0,
            tiled=True,
        ),
    )
    first_cos, first_sin = angle_table(
        jnp.arange(radix, dtype=jnp.int32), jnp.arange(seq_size, dtype=jnp.int32), radix
    )
    offsets = seq_index * block_rows + jnp.arange(block_rows, dtype=jnp.int32)
    turn_cos, turn_sin = angle_table(jnp.arange(radix, dtype=jnp.int32), offsets, full_len)
    sectioned = []
    for column_data in (sig_cols, filt_cols):
        part_re = jnp.einsum("kp,pqc->kqc", first_cos, column_data, precision=HIGHEST_PREC)
        part_im = -jnp.einsum("kp,pqc->kqc", first_sin, column_data, precision=HIGHEST_PREC)
        turned_re, turned_im = rotate(
            part_re, part_im, turn_cos[:, :, None], turn_sin[:, :, None], -1.0
        )
        sectioned.append(turned_re.reshape(seq_size, 2, block_rows, channel_count))
        sectioned.append(turned_im.reshape(seq_size, 2, block_rows, channel_count))
    back_re, back_im = spectral(
        (
            lax.all_to_all(sectioned[0], "seq", split_axis=0, concat_axis=2, tiled=True),
            lax.all_to_all(sectioned[1], "seq", split_axis=0, concat_axis=2, tiled=True),
            lax.all_to_all(sectioned[2], "seq", split_axis=0, concat_axis=2, tiled=True),
            lax.all_to_all(sectioned[3], "seq", split_axis=0, concat_axis=2, tiled=True),
        )
    )
    own_freq = 2 * seq_index + jnp.arange(2, dtype=jnp.int32)
    inv_cos, inv_sin = angle_table(own_freq, positions, full_len)
    inner_re, inner_im = rotate(
        back_re[0], back_im[0], inv_cos[:, :, None], inv_sin[:, :, None], 1.0
    )
    gathered_re, gathered_im = (
        lax.all_to_all(inner_re, "seq", split_axis=1, concat_axis=0, tiled=True),
        lax.all_to_all(inner_im, "seq", split_axis=1, concat_axis=0, tiled=True),
    )
    last_cos, last_sin = angle_table(
        jnp.arange(seq_size, dtype=jnp.int32), jnp.arange(radix, dtype=jnp.int32), radix
    )
    rows_part = (
        jnp.einsum("pk,kqc->pqc", last_cos, gathered_re, precision=HIGHEST_PREC)
        - jnp.einsum("pk,kqc->pqc", last_sin, gathered_im, precision=HIGHEST_PREC)
    ) / full_len
    conv = lax.all_to_all(rows_part, "seq", split_axis=0, concat_axis=1, tiled=True).reshape(
        row_count, channel_count
    )
    gated = (out_gate * (conv + skip_gain[None, :] * signal)).astype(jnp.bfloat16)
    whole = lax.all_gather(gated, "ch", axis=1, tiled=True)
    return jnp.dot(whole, out_weight, preferred_element_type=jnp.float32).astype(jnp.bfloat16)


DENSE_LIMIT = 2048


def half_step_tables(total):
    index = np.arange(total, dtype=np.int64)
    product = (2 * index[:, None] + 1) * index[None, :] % (4 * total)
    angle = 2.0 * np.pi / (4 * total) * product
    return np.cos(angle), np.sin(angle)


def dot32(left, right):
    return jnp.dot(left.astype(jnp.bfloat16), right.astype(jnp.bfloat16), preferred_element_type=jnp.float32)


def per_device(tokens, in_weight, filter_taps, skip_gain, out_weight):
    row_count, channel_count = filter_taps.shape
    seq_size = lax.axis_size("seq")
    seq_index = lax.axis_index("seq")
    own = channel_count // seq_size
    total = row_count * seq_size
    cos_table, sin_table = half_step_tables(total)
    table = jnp.asarray(np.concatenate([cos_table, sin_table]), jnp.bfloat16)
    back = jnp.asarray(np.concatenate([cos_table.T, -sin_table.T], axis=1) / total, jnp.bfloat16)
    all_tokens = lax.all_gather(tokens, "seq", axis=0, tiled=True)
    weight = lax.all_to_all(
        in_weight.reshape(-1, 3, seq_size, own).transpose(2, 0, 1, 3).reshape(seq_size, -1, 128),
        "seq", split_axis=0, concat_axis=0, tiled=True,
    ).reshape(all_tokens.shape[1], 3 * own)
    taps = lax.all_to_all(
        filter_taps.astype(jnp.bfloat16).reshape(row_count, seq_size, own).transpose(1, 0, 2).reshape(seq_size, -1, 128),
        "seq", split_axis=0, concat_axis=0, tiled=True,
    ).reshape(total, own)
    gain = lax.dynamic_slice_in_dim(skip_gain, seq_index * own, own)
    projected = jnp.dot(all_tokens, weight, preferred_element_type=jnp.float32).astype(jnp.bfloat16)
    values, in_gate, out_gate = (
        projected[:, j * own : (j + 1) * own].astype(jnp.float32) for j in range(3)
    )
    signal = in_gate * values
    spec = dot32(table, signal)
    resp = dot32(table, taps)
    spec_re, spec_im, resp_re, resp_im = spec[:total], spec[total:], resp[:total], resp[total:]
    prod = jnp.concatenate(
        [spec_re * resp_re - spec_im * resp_im, -(spec_re * resp_im + spec_im * resp_re)]
    )
    conv = dot32(back, prod)
    gated = (out_gate * (conv + gain[None, :] * signal)).astype(jnp.bfloat16)
    mine = lax.all_to_all(gated.reshape(seq_size, row_count * own // 128, 128), "seq", split_axis=0, concat_axis=0, tiled=True)
    whole = lax.all_gather(mine, "ch", axis=0, tiled=True)
    whole = whole.reshape(-1, row_count, own).transpose(1, 0, 2).reshape(row_count, -1)
    return jnp.dot(whole, out_weight, preferred_element_type=jnp.float32).astype(jnp.bfloat16)


def fused_kernel(
    tokens, weight, taps, gain, out_weight, table_hbm, back_hbm, out,
    all_tokens, pack_w, recv_w, full_w, pack_f, recv_f, all_taps, table, back, mix_w,
    resp, signal, split, out_gate, prod, pack_g, recv_g, wide,
    local_sem, w_send, w_recv, f_send, f_recv, up_send, down_send, z_recv, y_send, y_recv,
    c_send, c_recv, x_send, x_recv, k_send, k_recv, g_send, g_recv, h_send, h_recv,
):
    f32, bf16 = jnp.float32, jnp.bfloat16
    me, ch = lax.axis_index("seq"), lax.axis_index("ch")
    z, y = me // 2, me % 2
    rows, depth = tokens.shape[0], tokens.shape[1]
    part = rows // 4
    total = rows * 8
    half = rows // 2
    w_rows = weight.shape[0]
    chans = weight.shape[1] // 3
    own = chans // 8

    def flip(value, bit):
        return value + bit - 2 * bit * (value // bit % 2)

    x_ch, c_ch, d_ch = flip(ch, 2), flip(ch, 1), flip(flip(ch, 2), 1)
    mates = (c_ch, x_ch, d_ch)

    barrier = pltpu.get_barrier_semaphore()
    for k in range(1, 8):
        pl.semaphore_signal(
            barrier, inc=1, device_id={"seq": (me + k) % 8, "ch": ch},
            device_id_type=pl.DeviceIdType.MESH,
        )
    for mate in mates:
        pl.semaphore_signal(
            barrier, inc=1, device_id={"seq": me, "ch": mate}, device_id_type=pl.DeviceIdType.MESH
        )

    own_rows = pl.ds(pl.multiple_of(me * rows, rows), rows)
    loads = [
        pltpu.make_async_copy(tokens, all_tokens.at[own_rows, :], local_sem.at[0]),
        pltpu.make_async_copy(table_hbm, table, local_sem.at[1]),
        pltpu.make_async_copy(back_hbm, back, local_sem.at[2]),
        pltpu.make_async_copy(out_weight, mix_w, local_sem.at[3]),
    ]

    for p in range(8):
        lanes = slice(p * own, (p + 1) * own)
        pack_f[p] = jnp.concatenate([taps[:half, lanes], taps[half:, lanes]], axis=1).astype(bf16)
        pack_w[p, :w_rows] = jnp.concatenate(
            [weight[:, lanes], weight[:, chans + p * own : chans + (p + 1) * own]], axis=1
        )
        last = slice(2 * chans + p * own, 2 * chans + (p + 1) * own)
        pack_w[p, w_rows:] = jnp.concatenate(
            [weight[: w_rows // 2, last], weight[w_rows // 2 :, last]], axis=1
        )

    pl.semaphore_wait(barrier, 10)

    def remote(source, target, send, recv, seq_id, ch_id):
        return pltpu.make_async_remote_copy(
            src_ref=source, dst_ref=target, send_sem=send, recv_sem=recv,
            device_id={"seq": seq_id, "ch": ch_id}, device_id_type=pl.DeviceIdType.MESH,
        )

    def piece(seq_id, quarter):
        start = pl.multiple_of(seq_id * rows + quarter * part, part)
        return all_tokens.at[pl.ds(start, part), :]

    mine = tokens.at[pl.ds(pl.multiple_of(ch * part, part), part), :]

    def guarded(condition, action):
        if condition is None:
            action()
        else:
            pl.when(condition)(action)

    sent = []

    def send(condition, copy):
        guarded(condition, lambda: copy().start())
        sent.append((condition, copy))

    def z_copy(source, zs, step):
        sems = up_send if step > 0 else down_send
        return lambda: remote(source(), piece(2 * zs + y, ch), sems.at[zs], z_recv.at[zs], me + 2 * step, ch)

    def y_copy(source, zs):
        return lambda: remote(source(), piece(2 * zs + y, ch), y_send.at[zs], y_recv.at[zs], flip(me, 1), ch)

    send(z < 3, z_copy(lambda: mine, z, 1))
    send(z > 0, z_copy(lambda: mine, z, -1))
    send(None, y_copy(lambda: mine, z))

    def w_copy(k):
        p = (me + k) % 8
        return lambda: remote(pack_w.at[p], recv_w.at[me], w_send.at[k], w_recv.at[me], p, ch)

    def f_copy(k):
        p = (me + k) % 8
        return lambda: remote(pack_f.at[p], recv_f.at[me], f_send.at[k], f_recv.at[me], p, ch)

    order = (4, 3, 5, 2, 6, 1, 7)
    for k in order:
        send(None, f_copy(k))
    for k in order:
        send(None, w_copy(k))
    for load in loads:
        load.start()
    recv_w[me] = pack_w[me]
    recv_f[me] = pack_f[me]

    def spread(condition, s):
        send(condition, lambda: remote(piece(s, ch), piece(s, ch), c_send.at[s], c_recv.at[s], me, c_ch))
        send(condition, lambda: remote(piece(s, ch), piece(s, ch), x_send.at[s], x_recv.at[s], me, x_ch))

    def from_z(condition, zs, step):
        s = 2 * zs + y
        guarded(condition, lambda: z_copy(lambda: piece(s, ch), zs, step)().wait_recv())
        onward = (z < 3) if step > 0 else (z > 0)
        send(jnp.logical_and(condition, onward), z_copy(lambda: piece(s, ch), zs, step))
        send(condition, y_copy(lambda: piece(s, ch), zs))
        spread(condition, s)

    def from_y(condition, zs):
        s = 2 * zs + 1 - y
        guarded(condition, lambda: remote(
            piece(s, ch), piece(s, ch), y_send.at[zs], y_recv.at[zs], flip(me, 1), ch).wait_recv())
        spread(condition, s)

    def from_x(condition, s):
        guarded(condition, lambda: remote(
            piece(s, x_ch), piece(s, x_ch), x_send.at[s], x_recv.at[s], me, x_ch).wait_recv())
        send(condition, lambda: remote(
            piece(s, x_ch), piece(s, x_ch), k_send.at[s], k_recv.at[s], me, c_ch))

    from_y(None, z)
    arrived = [(None, 2 * z + 1 - y)]
    for d in range(1, 4):
        below, above = z >= d, z + d <= 3
        from_z(below, z - d, 1)
        from_z(above, z + d, -1)
        while arrived:
            from_x(*arrived.pop(0))
        from_y(below, z - d)
        from_y(above, z + d)
        for condition, zs in ((below, z - d), (above, z + d)):
            arrived += [(condition, 2 * zs + y), (condition, 2 * zs + 1 - y)]
        if d == 1:
            taps_phase(me, ch, remote, recv_f, f_send, f_recv, all_taps, half, own, loads, table, resp)
    while arrived:
        from_x(*arrived.pop(0))

    for k in range(1, 8):
        s = (me + k) % 8
        remote(recv_w.at[s], recv_w.at[s], w_send.at[k], w_recv.at[s], s, ch).wait_recv()
    for s in range(8):
        base = s * w_rows
        full_w[base : base + w_rows, : 2 * own] = recv_w[s, :w_rows]
        full_w[base : base + w_rows // 2, 2 * own :] = recv_w[s, w_rows:][:, :own]
        full_w[base + w_rows // 2 : base + w_rows, 2 * own :] = recv_w[s, w_rows:][:, own:]

    for k in range(1, 8):
        s = (me + k) % 8
        remote(piece(s, c_ch), piece(s, c_ch), c_send.at[s], c_recv.at[s], me, c_ch).wait_recv()
        remote(piece(s, d_ch), piece(s, d_ch), k_send.at[s], k_recv.at[s], me, c_ch).wait_recv()
    loads[0].wait()

    @pl.loop(0, total // 256)
    def _(i):
        at = pl.ds(pl.multiple_of(i * 256, 256), 256)
        proj = jnp.dot(all_tokens[at, :], full_w[...], preferred_element_type=f32)
        proj = proj.astype(bf16).astype(f32)
        sig = proj[:, own : 2 * own] * proj[:, :own]
        signal[at, :] = sig
        out_gate[at, :] = proj[:, 2 * own :]
        high = sig.astype(bf16)
        split[at, :] = jnp.concatenate([high, (sig - high.astype(f32)).astype(bf16)], axis=1)

    @pl.loop(0, total // 256)
    def _(i):
        at = pl.ds(pl.multiple_of(i * 256, 256), 256)
        under = pl.ds(pl.multiple_of(total + i * 256, 256), 256)
        re = jnp.dot(table[at, :], split[...], preferred_element_type=f32)
        im = jnp.dot(table[under, :], split[...], preferred_element_type=f32)
        re, im = re[:, :own] + re[:, own:], im[:, :own] + im[:, own:]
        filt_re, filt_im = resp[at, :], resp[under, :]
        prod[at, :] = (re * filt_re - im * filt_im).astype(bf16)
        prod[under, :] = (re * filt_im + im * filt_re).astype(bf16)

    skip = jnp.zeros((1, own), f32)
    for p in range(8):
        skip = skip + jnp.where(me == p, gain[:, p * own : (p + 1) * own], 0.0)

    loads[2].wait()

    def g_copy(k):
        p = (me + k) % 8
        return lambda: remote(pack_g.at[p], recv_g.at[ch, me], g_send.at[k], g_recv.at[me], p, ch)

    for k in (4, 3, 5, 2, 6, 1, 7, 0):
        p = (me + k) % 8
        at = pl.ds(pl.multiple_of(p * rows, rows), rows)
        conv = jnp.dot(back[at, :], prod[...], preferred_element_type=f32)
        gated = (out_gate[at, :] * (conv + skip * signal[at, :])).astype(bf16)
        packed = jnp.concatenate([gated[:half], gated[half:]], axis=1)
        if k:
            pack_g[p] = packed
            send(None, g_copy(k))
        else:
            recv_g[ch, me] = packed

    def h_copy(j, s):
        return lambda: remote(recv_g.at[ch, s], recv_g.at[ch, s], h_send.at[j, s], h_recv.at[j, s], me, mates[j])

    for k in (0, 1, 7, 2, 6, 3, 5, 4):
        s = (me + k) % 8
        if k:
            remote(recv_g.at[ch, s], recv_g.at[ch, s], g_send.at[k], g_recv.at[s], s, ch).wait_recv()
        for j in (2, 1, 0):
            send(None, h_copy(j, s))
    loads[3].wait()
    for j in range(3):
        for s in range(8):
            remote(
                recv_g.at[mates[j], s], recv_g.at[mates[j], s], h_send.at[j, s], h_recv.at[j, s], me, mates[j]
            ).wait_recv()
    for c in range(4):
        for s in range(0, 8, 2):
            base = (c * 8 + s) * own
            a, b = recv_g[c, s], recv_g[c, s + 1]
            wide[:half, base : base + 2 * own] = jnp.concatenate([a[:, :own], b[:, :own]], axis=1)
            wide[half:, base : base + 2 * own] = jnp.concatenate([a[:, own:], b[:, own:]], axis=1)
    out[...] = jnp.dot(wide[...], mix_w[...], preferred_element_type=f32).astype(bf16)
    for condition, copy in sent:
        guarded(condition, lambda copy=copy: copy().wait_send())


def taps_phase(me, ch, remote, recv_f, f_send, f_recv, all_taps, half, own, loads, table, resp):
    for k in range(1, 8):
        s = (me + k) % 8
        remote(recv_f.at[s], recv_f.at[s], f_send.at[k], f_recv.at[s], s, ch).wait_recv()
    for s in range(8):
        base = 2 * s * half
        all_taps[base : base + half, :] = recv_f[s][:, :own]
        all_taps[base + half : base + 2 * half, :] = recv_f[s][:, own:]
    loads[1].wait()

    @pl.loop(0, table.shape[0] // 256)
    def _(i):
        at = pl.ds(pl.multiple_of(i * 256, 256), 256)
        resp[at, :] = jnp.dot(table[at, :], all_taps[...], preferred_element_type=jnp.float32)


def per_device_fused(tokens, in_weight, filter_taps, skip_gain, out_weight):
    rows, depth = tokens.shape
    w_rows, _, chans = in_weight.shape
    own = chans // 8
    total = 8 * rows
    width = out_weight.shape[1]
    cos_table, sin_table = half_step_tables(total)
    table = jnp.asarray(np.concatenate([cos_table, sin_table]), jnp.bfloat16)
    back = jnp.asarray(np.concatenate([cos_table.T, sin_table.T], axis=1) / total, jnp.bfloat16)
    f32, bf16 = jnp.float32, jnp.bfloat16
    vmem, anywhere = pl.BlockSpec(memory_space=pltpu.VMEM), pl.BlockSpec(memory_space=pl.ANY)
    dma = pltpu.SemaphoreType.DMA
    return pl.pallas_call(
        fused_kernel,
        out_shape=jax.ShapeDtypeStruct((rows, width), bf16),
        in_specs=[anywhere, vmem, vmem, vmem, anywhere, anywhere, anywhere],
        out_specs=vmem,
        scratch_shapes=[
            pltpu.VMEM((total, depth), bf16),
            pltpu.VMEM((8, w_rows * 3 // 2, 2 * own), bf16),
            pltpu.VMEM((8, w_rows * 3 // 2, 2 * own), bf16),
            pltpu.VMEM((8 * w_rows, 3 * own), bf16),
            pltpu.VMEM((8, rows // 2, 2 * own), bf16),
            pltpu.VMEM((8, rows // 2, 2 * own), bf16),
            pltpu.VMEM((total, own), bf16),
            pltpu.VMEM((2 * total, total), bf16),
            pltpu.VMEM((total, 2 * total), bf16),
            pltpu.VMEM(out_weight.shape, bf16),
            pltpu.VMEM((2 * total, own), f32),
            pltpu.VMEM((total, own), f32),
            pltpu.VMEM((total, 2 * own), bf16),
            pltpu.VMEM((total, own), f32),
            pltpu.VMEM((2 * total, own), bf16),
            pltpu.VMEM((8, rows // 2, 2 * own), bf16),
            pltpu.VMEM((4, 8, rows // 2, 2 * own), bf16),
            pltpu.VMEM((rows, out_weight.shape[0]), bf16),
            dma((4,)), dma((8,)), dma((8,)), dma((8,)), dma((8,)),
            dma((4,)), dma((4,)), dma((4,)), dma((4,)), dma((4,)),
            dma((8,)), dma((8,)), dma((8,)), dma((8,)), dma((8,)), dma((8,)),
            dma((8,)), dma((8,)), dma((3, 8)), dma((3, 8)),
        ],
        compiler_params=pltpu.CompilerParams(
            collective_id=0, has_side_effects=True, vmem_limit_bytes=50 * 2**20
        ),
    )(
        tokens, in_weight.reshape(w_rows, 3 * chans), filter_taps, skip_gain[None, :],
        out_weight, table, back,
    )


def solution(mesh):
    in_specs = (P("seq", None), P("seq", None, "ch"), P("seq", "ch"), P("ch"), P(None, "ch"))
    out_specs = P("seq", "ch")

    def whole(tokens, in_weight, filter_taps, skip_gain, out_weight):
        fits = mesh.shape["seq"] == 8 and mesh.shape["ch"] == 4
        fits = fits and tokens.shape[0] == 1024 and filter_taps.shape[1] == 2048
        if fits:
            body = per_device_fused
        else:
            body = per_device if tokens.shape[0] <= DENSE_LIMIT else per_device_long
        return jax.shard_map(
            body, mesh=mesh, in_specs=in_specs, out_specs=out_specs, check_vma=False
        )(tokens, in_weight, filter_taps, skip_gain, out_weight)

    return whole
```

```python
import functools
import math

import jax
import jax.numpy as jnp
import numpy as np
from jax import lax
from jax.experimental import pallas as pl
from jax.experimental.pallas import tpu as pltpu
from jax.sharding import PartitionSpec as P

HIGHEST_PREC = lax.Precision.HIGHEST


def angle_table(first_index, second_index, period):
    product = first_index[:, None] * second_index[None, :] % period
    angle = 2.0 * math.pi / period * product.astype(jnp.float32)
    return (jnp.cos(angle), jnp.sin(angle))


def contract(matrix, blocks):
    return jnp.einsum("kn,...nc->...kc", matrix, blocks, precision=HIGHEST_PREC)


def rotate(real_part, imag_part, cosine, sine, direction):
    return (
        real_part * cosine - direction * imag_part * sine,
        imag_part * cosine + direction * real_part * sine,
    )


def spectral(parts):
    sig_re, sig_im, filt_re, filt_im = parts
    row_count = sig_re.shape[-2]
    index = jnp.arange(row_count, dtype=jnp.int32)
    cosine, sine = angle_table(index, index, row_count)

    def forward(real_part, imag_part):
        return (
            contract(cosine, real_part) + contract(sine, imag_part),
            contract(cosine, imag_part) - contract(sine, real_part),
        )

    spec_re, spec_im = forward(sig_re, sig_im)
    resp_re, resp_im = forward(filt_re, filt_im)
    prod_re = spec_re * resp_re - spec_im * resp_im
    prod_im = spec_re * resp_im + spec_im * resp_re
    return (
        contract(cosine, prod_re) - contract(sine, prod_im),
        contract(cosine, prod_im) + contract(sine, prod_re),
    )


def per_device_long(tokens, in_weight, filter_taps, skip_gain, out_weight):
    row_count, channel_count = filter_taps.shape
    seq_size = lax.axis_size("seq")
    seq_index = lax.axis_index("seq")
    full_len = 2 * seq_size * row_count
    radix = 2 * seq_size
    positions = jnp.arange(row_count, dtype=jnp.int32)
    piece = lax.all_gather(in_weight, "seq", axis=0, tiled=True)
    width_rows = piece.shape[0]
    projected = jnp.dot(
        tokens, piece.reshape(width_rows, 3 * channel_count), preferred_element_type=jnp.float32
    )
    projected = projected.astype(jnp.bfloat16).reshape(row_count, 3, channel_count)
    values = projected[:, 0].astype(jnp.float32)
    in_gate = projected[:, 1].astype(jnp.float32)
    out_gate = projected[:, 2].astype(jnp.float32)
    signal = in_gate * values
    block_rows = row_count // seq_size
    sig_cols, filt_cols = (
        lax.all_to_all(
            signal.reshape(1, row_count, channel_count),
            "seq",
            split_axis=1,
            concat_axis=0,
            tiled=True,
        ),
        lax.all_to_all(
            filter_taps.reshape(1, row_count, channel_count),
            "seq",
            split_axis=1,
            concat_axis=0,
            tiled=True,
        ),
    )
    first_cos, first_sin = angle_table(
        jnp.arange(radix, dtype=jnp.int32), jnp.arange(seq_size, dtype=jnp.int32), radix
    )
    offsets = seq_index * block_rows + jnp.arange(block_rows, dtype=jnp.int32)
    turn_cos, turn_sin = angle_table(jnp.arange(radix, dtype=jnp.int32), offsets, full_len)
    sectioned = []
    for column_data in (sig_cols, filt_cols):
        part_re = jnp.einsum("kp,pqc->kqc", first_cos, column_data, precision=HIGHEST_PREC)
        part_im = -jnp.einsum("kp,pqc->kqc", first_sin, column_data, precision=HIGHEST_PREC)
        turned_re, turned_im = rotate(
            part_re, part_im, turn_cos[:, :, None], turn_sin[:, :, None], -1.0
        )
        sectioned.append(turned_re.reshape(seq_size, 2, block_rows, channel_count))
        sectioned.append(turned_im.reshape(seq_size, 2, block_rows, channel_count))
    back_re, back_im = spectral(
        (
            lax.all_to_all(sectioned[0], "seq", split_axis=0, concat_axis=2, tiled=True),
            lax.all_to_all(sectioned[1], "seq", split_axis=0, concat_axis=2, tiled=True),
            lax.all_to_all(sectioned[2], "seq", split_axis=0, concat_axis=2, tiled=True),
            lax.all_to_all(sectioned[3], "seq", split_axis=0, concat_axis=2, tiled=True),
        )
    )
    own_freq = 2 * seq_index + jnp.arange(2, dtype=jnp.int32)
    inv_cos, inv_sin = angle_table(own_freq, positions, full_len)
    inner_re, inner_im = rotate(
        back_re[0], back_im[0], inv_cos[:, :, None], inv_sin[:, :, None], 1.0
    )
    gathered_re, gathered_im = (
        lax.all_to_all(inner_re, "seq", split_axis=1, concat_axis=0, tiled=True),
        lax.all_to_all(inner_im, "seq", split_axis=1, concat_axis=0, tiled=True),
    )
    last_cos, last_sin = angle_table(
        jnp.arange(seq_size, dtype=jnp.int32), jnp.arange(radix, dtype=jnp.int32), radix
    )
    rows_part = (
        jnp.einsum("pk,kqc->pqc", last_cos, gathered_re, precision=HIGHEST_PREC)
        - jnp.einsum("pk,kqc->pqc", last_sin, gathered_im, precision=HIGHEST_PREC)
    ) / full_len
    conv = lax.all_to_all(rows_part, "seq", split_axis=0, concat_axis=1, tiled=True).reshape(
        row_count, channel_count
    )
    gated = (out_gate * (conv + skip_gain[None, :] * signal)).astype(jnp.bfloat16)
    whole = lax.all_gather(gated, "ch", axis=1, tiled=True)
    return jnp.dot(whole, out_weight, preferred_element_type=jnp.float32).astype(jnp.bfloat16)


DENSE_LIMIT = 2048


def half_step_tables(total):
    index = np.arange(total, dtype=np.int64)
    product = (2 * index[:, None] + 1) * index[None, :] % (4 * total)
    angle = 2.0 * np.pi / (4 * total) * product
    return np.cos(angle), np.sin(angle)


def dot32(left, right):
    return jnp.dot(left.astype(jnp.bfloat16), right.astype(jnp.bfloat16), preferred_element_type=jnp.float32)


def per_device(tokens, in_weight, filter_taps, skip_gain, out_weight):
    row_count, channel_count = filter_taps.shape
    seq_size = lax.axis_size("seq")
    seq_index = lax.axis_index("seq")
    own = channel_count // seq_size
    total = row_count * seq_size
    cos_table, sin_table = half_step_tables(total)
    table = jnp.asarray(np.concatenate([cos_table, sin_table]), jnp.bfloat16)
    back = jnp.asarray(np.concatenate([cos_table.T, -sin_table.T], axis=1) / total, jnp.bfloat16)
    all_tokens = lax.all_gather(tokens, "seq", axis=0, tiled=True)
    weight = lax.all_to_all(
        in_weight.reshape(-1, 3, seq_size, own).transpose(2, 0, 1, 3).reshape(seq_size, -1, 128),
        "seq", split_axis=0, concat_axis=0, tiled=True,
    ).reshape(all_tokens.shape[1], 3 * own)
    taps = lax.all_to_all(
        filter_taps.astype(jnp.bfloat16).reshape(row_count, seq_size, own).transpose(1, 0, 2).reshape(seq_size, -1, 128),
        "seq", split_axis=0, concat_axis=0, tiled=True,
    ).reshape(total, own)
    gain = lax.dynamic_slice_in_dim(skip_gain, seq_index * own, own)
    projected = jnp.dot(all_tokens, weight, preferred_element_type=jnp.float32).astype(jnp.bfloat16)
    values, in_gate, out_gate = (
        projected[:, j * own : (j + 1) * own].astype(jnp.float32) for j in range(3)
    )
    signal = in_gate * values
    spec = dot32(table, signal)
    resp = dot32(table, taps)
    spec_re, spec_im, resp_re, resp_im = spec[:total], spec[total:], resp[:total], resp[total:]
    prod = jnp.concatenate(
        [spec_re * resp_re - spec_im * resp_im, -(spec_re * resp_im + spec_im * resp_re)]
    )
    conv = dot32(back, prod)
    gated = (out_gate * (conv + gain[None, :] * signal)).astype(jnp.bfloat16)
    mine = lax.all_to_all(gated.reshape(seq_size, row_count * own // 128, 128), "seq", split_axis=0, concat_axis=0, tiled=True)
    whole = lax.all_gather(mine, "ch", axis=0, tiled=True)
    whole = whole.reshape(-1, row_count, own).transpose(1, 0, 2).reshape(row_count, -1)
    return jnp.dot(whole, out_weight, preferred_element_type=jnp.float32).astype(jnp.bfloat16)


def fused_kernel(
    tokens, weight_hbm, taps_hbm, gain_hbm, out_weight, table_hbm, back_hbm, out,
    weight, taps, gain,
    all_tokens, pack_w, recv_w, full_w, pack_f, recv_f, all_taps, table, back, mix_w,
    resp, signal, split, out_gate, prod, pack_g, recv_g, wide,
    local_sem, w_send, w_recv, f_send, f_recv, up_send, down_send, z_recv, y_send, y_recv,
    c_send, c_recv, x_send, x_recv, k_send, k_recv, g_send, g_recv, h_send, h_recv,
):
    f32, bf16 = jnp.float32, jnp.bfloat16
    me, ch = lax.axis_index("seq"), lax.axis_index("ch")
    z, y = me // 2, me % 2
    rows, depth = tokens.shape[0], tokens.shape[1]
    part = rows // 4
    total = rows * 8
    half = rows // 2
    w_rows, chans = weight.shape[1:]
    own = chans // 8

    def flip(value, bit):
        return value + bit - 2 * bit * (value // bit % 2)

    x_ch, c_ch, d_ch = flip(ch, 2), flip(ch, 1), flip(flip(ch, 2), 1)
    mates = (c_ch, x_ch, d_ch)

    first_loads = [
        pltpu.make_async_copy(weight_hbm, weight, local_sem.at[4]),
        pltpu.make_async_copy(taps_hbm, taps, local_sem.at[5]),
        pltpu.make_async_copy(gain_hbm, gain, local_sem.at[6]),
    ]
    for load in first_loads:
        load.start()
    barrier = pltpu.get_barrier_semaphore()
    for k in range(1, 8):
        pl.semaphore_signal(
            barrier, inc=1, device_id={"seq": (me + k) % 8, "ch": ch},
            device_id_type=pl.DeviceIdType.MESH,
        )
    for mate in mates:
        pl.semaphore_signal(
            barrier, inc=1, device_id={"seq": me, "ch": mate}, device_id_type=pl.DeviceIdType.MESH
        )

    own_rows = pl.ds(pl.multiple_of(me * rows, rows), rows)
    loads = [
        pltpu.make_async_copy(tokens, all_tokens.at[own_rows, :], local_sem.at[0]),
        pltpu.make_async_copy(table_hbm, table, local_sem.at[1]),
        pltpu.make_async_copy(back_hbm, back, local_sem.at[2]),
        pltpu.make_async_copy(out_weight, mix_w, local_sem.at[3]),
    ]

    for load in first_loads:
        load.wait()
    for p in range(8):
        lanes = slice(p * own, (p + 1) * own)
        pack_f[p] = jnp.concatenate([taps[:half, lanes], taps[half:, lanes]], axis=1).astype(bf16)
        pack_w[p, :w_rows] = jnp.concatenate([weight[0, :, lanes], weight[1, :, lanes]], axis=1)
        pack_w[p, w_rows:] = jnp.concatenate(
            [weight[2, : w_rows // 2, lanes], weight[2, w_rows // 2 :, lanes]], axis=1
        )

    pl.semaphore_wait(barrier, 10)

    def remote(source, target, send, recv, seq_id, ch_id):
        return pltpu.make_async_remote_copy(
            src_ref=source, dst_ref=target, send_sem=send, recv_sem=recv,
            device_id={"seq": seq_id, "ch": ch_id}, device_id_type=pl.DeviceIdType.MESH,
        )

    def piece(seq_id, quarter):
        start = pl.multiple_of(seq_id * rows + quarter * part, part)
        return all_tokens.at[pl.ds(start, part), :]

    mine = tokens.at[pl.ds(pl.multiple_of(ch * part, part), part), :]

    def guarded(condition, action):
        if condition is None:
            action()
        else:
            pl.when(condition)(action)

    sent = []

    def send(condition, copy):
        guarded(condition, lambda: copy().start())
        sent.append((condition, copy))

    def z_copy(source, zs, step):
        sems = up_send if step > 0 else down_send
        return lambda: remote(source(), piece(2 * zs + y, ch), sems.at[zs], z_recv.at[zs], me + 2 * step, ch)

    def y_copy(source, zs):
        return lambda: remote(source(), piece(2 * zs + y, ch), y_send.at[zs], y_recv.at[zs], flip(me, 1), ch)

    send(z < 3, z_copy(lambda: mine, z, 1))
    send(z > 0, z_copy(lambda: mine, z, -1))
    send(None, y_copy(lambda: mine, z))

    def w_copy(k):
        p = (me + k) % 8
        return lambda: remote(pack_w.at[p], recv_w.at[me], w_send.at[k], w_recv.at[me], p, ch)

    def f_copy(k):
        p = (me + k) % 8
        return lambda: remote(pack_f.at[p], recv_f.at[me], f_send.at[k], f_recv.at[me], p, ch)

    order = (4, 3, 5, 2, 6, 1, 7)
    for k in order:
        send(None, f_copy(k))
    pending = list(order)

    def more(count):
        for k in pending[:count]:
            send(None, w_copy(k))
        del pending[:count]

    more(1)
    for load in loads:
        load.start()
    recv_w[me] = pack_w[me]
    recv_f[me] = pack_f[me]

    def spread(condition, s):
        send(condition, lambda: remote(piece(s, ch), piece(s, ch), c_send.at[s], c_recv.at[s], me, c_ch))
        send(condition, lambda: remote(piece(s, ch), piece(s, ch), x_send.at[s], x_recv.at[s], me, x_ch))

    def from_z(condition, zs, step):
        s = 2 * zs + y
        guarded(condition, lambda: z_copy(lambda: piece(s, ch), zs, step)().wait_recv())
        onward = (z < 3) if step > 0 else (z > 0)
        send(jnp.logical_and(condition, onward), z_copy(lambda: piece(s, ch), zs, step))
        send(condition, y_copy(lambda: piece(s, ch), zs))
        spread(condition, s)

    def from_y(condition, zs):
        s = 2 * zs + 1 - y
        guarded(condition, lambda: remote(
            piece(s, ch), piece(s, ch), y_send.at[zs], y_recv.at[zs], flip(me, 1), ch).wait_recv())
        spread(condition, s)

    def from_x(condition, s):
        guarded(condition, lambda: remote(
            piece(s, x_ch), piece(s, x_ch), x_send.at[s], x_recv.at[s], me, x_ch).wait_recv())
        send(condition, lambda: remote(
            piece(s, x_ch), piece(s, x_ch), k_send.at[s], k_recv.at[s], me, c_ch))

    tiles = [functools.partial(taps_tile, i, table, all_taps, resp) for i in range(8)]
    from_y(None, z)
    more(1)
    arrived = [(None, 2 * z + 1 - y)]
    for d in range(1, 4):
        below, above = z >= d, z + d <= 3
        from_z(below, z - d, 1)
        from_z(above, z + d, -1)
        more(1)
        if d == 1:
            taps_arrive(me, ch, remote, recv_f, f_send, f_recv, all_taps, half, own)
            loads[1].wait()
        else:
            tiles.pop(0)()
        from_y(below, z - d)
        tiles.pop(0)()
        from_y(above, z + d)
        more(1)
        tiles.pop(0)()
        for condition, zs in ((below, z - d), (above, z + d)):
            arrived += [(condition, 2 * zs + y), (condition, 2 * zs + 1 - y)]
    while arrived:
        from_x(*arrived.pop(0))
    while tiles:
        tiles.pop(0)()

    for k in range(1, 8):
        s = (me + k) % 8
        remote(recv_w.at[s], recv_w.at[s], w_send.at[k], w_recv.at[s], s, ch).wait_recv()
    for s in range(8):
        base = s * w_rows
        full_w[base : base + w_rows, : 2 * own] = recv_w[s, :w_rows]
        full_w[base : base + w_rows // 2, 2 * own :] = recv_w[s, w_rows:][:, :own]
        full_w[base + w_rows // 2 : base + w_rows, 2 * own :] = recv_w[s, w_rows:][:, own:]

    for k in range(1, 8):
        s = (me + k) % 8
        remote(piece(s, c_ch), piece(s, c_ch), c_send.at[s], c_recv.at[s], me, c_ch).wait_recv()
        remote(piece(s, d_ch), piece(s, d_ch), k_send.at[s], k_recv.at[s], me, c_ch).wait_recv()
    loads[0].wait()

    @pl.loop(0, total // 256)
    def _(i):
        at = pl.ds(pl.multiple_of(i * 256, 256), 256)
        proj = jnp.dot(all_tokens[at, :], full_w[...], preferred_element_type=f32)
        proj = proj.astype(bf16).astype(f32)
        sig = proj[:, own : 2 * own] * proj[:, :own]
        signal[at, :] = sig
        out_gate[at, :] = proj[:, 2 * own :]
        high = sig.astype(bf16)
        split[at, :] = jnp.concatenate([high, (sig - high.astype(f32)).astype(bf16)], axis=1)

    @pl.loop(0, total // 256)
    def _(i):
        at = pl.ds(pl.multiple_of(i * 256, 256), 256)
        under = pl.ds(pl.multiple_of(total + i * 256, 256), 256)
        re = jnp.dot(table[at, :], split[...], preferred_element_type=f32)
        im = jnp.dot(table[under, :], split[...], preferred_element_type=f32)
        re, im = re[:, :own] + re[:, own:], im[:, :own] + im[:, own:]
        filt_re, filt_im = resp[at, :], resp[under, :]
        prod[at, :] = (re * filt_re - im * filt_im).astype(bf16)
        prod[under, :] = (re * filt_im + im * filt_re).astype(bf16)

    skip = jnp.zeros((1, own), f32)
    for p in range(8):
        skip = skip + jnp.where(me == p, gain[:, p * own : (p + 1) * own], 0.0)

    loads[2].wait()

    def g_copy(k):
        p = (me + k) % 8
        return lambda: remote(pack_g.at[p], recv_g.at[ch, me], g_send.at[k], g_recv.at[me], p, ch)

    for k in (4, 3, 5, 2, 6, 1, 7, 0):
        p = (me + k) % 8
        at = pl.ds(pl.multiple_of(p * rows, rows), rows)
        conv = jnp.dot(back[at, :], prod[...], preferred_element_type=f32)
        gated = (out_gate[at, :] * (conv + skip * signal[at, :])).astype(bf16)
        packed = jnp.concatenate([gated[:half], gated[half:]], axis=1)
        if k:
            pack_g[p] = packed
            send(None, g_copy(k))
        else:
            recv_g[ch, me] = packed

    def h_copy(j, s):
        return lambda: remote(recv_g.at[ch, s], recv_g.at[ch, s], h_send.at[j, s], h_recv.at[j, s], me, mates[j])

    for k in (0, 1, 7, 2, 6, 3, 5, 4):
        s = (me + k) % 8
        if k:
            remote(recv_g.at[ch, s], recv_g.at[ch, s], g_send.at[k], g_recv.at[s], s, ch).wait_recv()
        for j in (2, 1, 0):
            send(None, h_copy(j, s))
    loads[3].wait()
    for j in range(3):
        for s in range(8):
            remote(
                recv_g.at[mates[j], s], recv_g.at[mates[j], s], h_send.at[j, s], h_recv.at[j, s], me, mates[j]
            ).wait_recv()
    for c in range(4):
        for s in range(0, 8, 2):
            base = (c * 8 + s) * own
            a, b = recv_g[c, s], recv_g[c, s + 1]
            wide[:half, base : base + 2 * own] = jnp.concatenate([a[:, :own], b[:, :own]], axis=1)
            wide[half:, base : base + 2 * own] = jnp.concatenate([a[:, own:], b[:, own:]], axis=1)
    out[...] = jnp.dot(wide[...], mix_w[...], preferred_element_type=f32).astype(bf16)
    for condition, copy in sent:
        guarded(condition, lambda copy=copy: copy().wait_send())


def taps_arrive(me, ch, remote, recv_f, f_send, f_recv, all_taps, half, own):
    for k in range(1, 8):
        s = (me + k) % 8
        remote(recv_f.at[s], recv_f.at[s], f_send.at[k], f_recv.at[s], s, ch).wait_recv()
    for s in range(8):
        base = 2 * s * half
        all_taps[base : base + half, :] = recv_f[s][:, :own]
        all_taps[base + half : base + 2 * half, :] = recv_f[s][:, own:]


def taps_tile(i, table, all_taps, resp):
    at = slice(i * 256, i * 256 + 256)
    resp[at, :] = jnp.dot(table[at, :], all_taps[...], preferred_element_type=jnp.float32)


def per_device_fused(tokens, in_weight, filter_taps, skip_gain, out_weight):
    rows, depth = tokens.shape
    w_rows, _, chans = in_weight.shape
    own = chans // 8
    total = 8 * rows
    width = out_weight.shape[1]
    cos_table, sin_table = half_step_tables(total)
    table = jnp.asarray(np.concatenate([cos_table, sin_table]), jnp.bfloat16)
    back = jnp.asarray(np.concatenate([cos_table.T, sin_table.T], axis=1) / total, jnp.bfloat16)
    f32, bf16 = jnp.float32, jnp.bfloat16
    vmem, anywhere = pl.BlockSpec(memory_space=pltpu.VMEM), pl.BlockSpec(memory_space=pl.ANY)
    dma = pltpu.SemaphoreType.DMA
    return pl.pallas_call(
        fused_kernel,
        out_shape=jax.ShapeDtypeStruct((rows, width), bf16),
        in_specs=[anywhere] * 7,
        out_specs=vmem,
        scratch_shapes=[
            pltpu.VMEM((3, w_rows, chans), bf16),
            pltpu.VMEM((rows, chans), f32),
            pltpu.VMEM((1, chans), f32),
            pltpu.VMEM((total, depth), bf16),
            pltpu.VMEM((8, w_rows * 3 // 2, 2 * own), bf16),
            pltpu.VMEM((8, w_rows * 3 // 2, 2 * own), bf16),
            pltpu.VMEM((8 * w_rows, 3 * own), bf16),
            pltpu.VMEM((8, rows // 2, 2 * own), bf16),
            pltpu.VMEM((8, rows // 2, 2 * own), bf16),
            pltpu.VMEM((total, own), bf16),
            pltpu.VMEM((2 * total, total), bf16),
            pltpu.VMEM((total, 2 * total), bf16),
            pltpu.VMEM(out_weight.shape, bf16),
            pltpu.VMEM((2 * total, own), f32),
            pltpu.VMEM((total, own), f32),
            pltpu.VMEM((total, 2 * own), bf16),
            pltpu.VMEM((total, own), f32),
            pltpu.VMEM((2 * total, own), bf16),
            pltpu.VMEM((8, rows // 2, 2 * own), bf16),
            pltpu.VMEM((4, 8, rows // 2, 2 * own), bf16),
            pltpu.VMEM((rows, out_weight.shape[0]), bf16),
            dma((7,)), dma((8,)), dma((8,)), dma((8,)), dma((8,)),
            dma((4,)), dma((4,)), dma((4,)), dma((4,)), dma((4,)),
            dma((8,)), dma((8,)), dma((8,)), dma((8,)), dma((8,)), dma((8,)),
            dma((8,)), dma((8,)), dma((3, 8)), dma((3, 8)),
        ],
        compiler_params=pltpu.CompilerParams(
            collective_id=0, has_side_effects=True, vmem_limit_bytes=60 * 2**20
        ),
    )(
        tokens, in_weight.transpose(1, 0, 2), filter_taps, skip_gain[None, :],
        out_weight, table, back,
    )


def solution(mesh):
    in_specs = (P("seq", None), P("seq", None, "ch"), P("seq", "ch"), P("ch"), P(None, "ch"))
    out_specs = P("seq", "ch")

    def whole(tokens, in_weight, filter_taps, skip_gain, out_weight):
        fits = mesh.shape["seq"] == 8 and mesh.shape["ch"] == 4
        fits = fits and tokens.shape[0] == 1024 and filter_taps.shape[1] == 2048
        if fits:
            body = per_device_fused
        else:
            body = per_device if tokens.shape[0] <= DENSE_LIMIT else per_device_long
        return jax.shard_map(
            body, mesh=mesh, in_specs=in_specs, out_specs=out_specs, check_vma=False
        )(tokens, in_weight, filter_taps, skip_gain, out_weight)

    return whole
```

```python
import functools
import math

import jax
import jax.numpy as jnp
import numpy as np
from jax import lax
from jax.experimental import pallas as pl
from jax.experimental.pallas import tpu as pltpu
from jax.sharding import PartitionSpec as P

HIGHEST_PREC = lax.Precision.HIGHEST


def angle_table(first_index, second_index, period):
    product = first_index[:, None] * second_index[None, :] % period
    angle = 2.0 * math.pi / period * product.astype(jnp.float32)
    return (jnp.cos(angle), jnp.sin(angle))


def contract(matrix, blocks):
    return jnp.einsum("kn,...nc->...kc", matrix, blocks, precision=HIGHEST_PREC)


def rotate(real_part, imag_part, cosine, sine, direction):
    return (
        real_part * cosine - direction * imag_part * sine,
        imag_part * cosine + direction * real_part * sine,
    )


def spectral(parts):
    sig_re, sig_im, filt_re, filt_im = parts
    row_count = sig_re.shape[-2]
    index = jnp.arange(row_count, dtype=jnp.int32)
    cosine, sine = angle_table(index, index, row_count)

    def forward(real_part, imag_part):
        return (
            contract(cosine, real_part) + contract(sine, imag_part),
            contract(cosine, imag_part) - contract(sine, real_part),
        )

    spec_re, spec_im = forward(sig_re, sig_im)
    resp_re, resp_im = forward(filt_re, filt_im)
    prod_re = spec_re * resp_re - spec_im * resp_im
    prod_im = spec_re * resp_im + spec_im * resp_re
    return (
        contract(cosine, prod_re) - contract(sine, prod_im),
        contract(cosine, prod_im) + contract(sine, prod_re),
    )


def per_device_long(tokens, in_weight, filter_taps, skip_gain, out_weight):
    row_count, channel_count = filter_taps.shape
    seq_size = lax.axis_size("seq")
    seq_index = lax.axis_index("seq")
    full_len = 2 * seq_size * row_count
    radix = 2 * seq_size
    positions = jnp.arange(row_count, dtype=jnp.int32)
    piece = lax.all_gather(in_weight, "seq", axis=0, tiled=True)
    width_rows = piece.shape[0]
    projected = jnp.dot(
        tokens, piece.reshape(width_rows, 3 * channel_count), preferred_element_type=jnp.float32
    )
    projected = projected.astype(jnp.bfloat16).reshape(row_count, 3, channel_count)
    values = projected[:, 0].astype(jnp.float32)
    in_gate = projected[:, 1].astype(jnp.float32)
    out_gate = projected[:, 2].astype(jnp.float32)
    signal = in_gate * values
    block_rows = row_count // seq_size
    sig_cols, filt_cols = (
        lax.all_to_all(
            signal.reshape(1, row_count, channel_count),
            "seq",
            split_axis=1,
            concat_axis=0,
            tiled=True,
        ),
        lax.all_to_all(
            filter_taps.reshape(1, row_count, channel_count),
            "seq",
            split_axis=1,
            concat_axis=0,
            tiled=True,
        ),
    )
    first_cos, first_sin = angle_table(
        jnp.arange(radix, dtype=jnp.int32), jnp.arange(seq_size, dtype=jnp.int32), radix
    )
    offsets = seq_index * block_rows + jnp.arange(block_rows, dtype=jnp.int32)
    turn_cos, turn_sin = angle_table(jnp.arange(radix, dtype=jnp.int32), offsets, full_len)
    sectioned = []
    for column_data in (sig_cols, filt_cols):
        part_re = jnp.einsum("kp,pqc->kqc", first_cos, column_data, precision=HIGHEST_PREC)
        part_im = -jnp.einsum("kp,pqc->kqc", first_sin, column_data, precision=HIGHEST_PREC)
        turned_re, turned_im = rotate(
            part_re, part_im, turn_cos[:, :, None], turn_sin[:, :, None], -1.0
        )
        sectioned.append(turned_re.reshape(seq_size, 2, block_rows, channel_count))
        sectioned.append(turned_im.reshape(seq_size, 2, block_rows, channel_count))
    back_re, back_im = spectral(
        (
            lax.all_to_all(sectioned[0], "seq", split_axis=0, concat_axis=2, tiled=True),
            lax.all_to_all(sectioned[1], "seq", split_axis=0, concat_axis=2, tiled=True),
            lax.all_to_all(sectioned[2], "seq", split_axis=0, concat_axis=2, tiled=True),
            lax.all_to_all(sectioned[3], "seq", split_axis=0, concat_axis=2, tiled=True),
        )
    )
    own_freq = 2 * seq_index + jnp.arange(2, dtype=jnp.int32)
    inv_cos, inv_sin = angle_table(own_freq, positions, full_len)
    inner_re, inner_im = rotate(
        back_re[0], back_im[0], inv_cos[:, :, None], inv_sin[:, :, None], 1.0
    )
    gathered_re, gathered_im = (
        lax.all_to_all(inner_re, "seq", split_axis=1, concat_axis=0, tiled=True),
        lax.all_to_all(inner_im, "seq", split_axis=1, concat_axis=0, tiled=True),
    )
    last_cos, last_sin = angle_table(
        jnp.arange(seq_size, dtype=jnp.int32), jnp.arange(radix, dtype=jnp.int32), radix
    )
    rows_part = (
        jnp.einsum("pk,kqc->pqc", last_cos, gathered_re, precision=HIGHEST_PREC)
        - jnp.einsum("pk,kqc->pqc", last_sin, gathered_im, precision=HIGHEST_PREC)
    ) / full_len
    conv = lax.all_to_all(rows_part, "seq", split_axis=0, concat_axis=1, tiled=True).reshape(
        row_count, channel_count
    )
    gated = (out_gate * (conv + skip_gain[None, :] * signal)).astype(jnp.bfloat16)
    whole = lax.all_gather(gated, "ch", axis=1, tiled=True)
    return jnp.dot(whole, out_weight, preferred_element_type=jnp.float32).astype(jnp.bfloat16)


DENSE_LIMIT = 2048


def half_step_tables(total):
    index = np.arange(total, dtype=np.int64)
    product = (2 * index[:, None] + 1) * index[None, :] % (4 * total)
    angle = 2.0 * np.pi / (4 * total) * product
    return np.cos(angle), np.sin(angle)


def dot32(left, right):
    return jnp.dot(left.astype(jnp.bfloat16), right.astype(jnp.bfloat16), preferred_element_type=jnp.float32)


def per_device(tokens, in_weight, filter_taps, skip_gain, out_weight):
    row_count, channel_count = filter_taps.shape
    seq_size = lax.axis_size("seq")
    seq_index = lax.axis_index("seq")
    own = channel_count // seq_size
    total = row_count * seq_size
    cos_table, sin_table = half_step_tables(total)
    table = jnp.asarray(np.concatenate([cos_table, sin_table]), jnp.bfloat16)
    back = jnp.asarray(np.concatenate([cos_table.T, -sin_table.T], axis=1) / total, jnp.bfloat16)
    all_tokens = lax.all_gather(tokens, "seq", axis=0, tiled=True)
    weight = lax.all_to_all(
        in_weight.reshape(-1, 3, seq_size, own).transpose(2, 0, 1, 3).reshape(seq_size, -1, 128),
        "seq", split_axis=0, concat_axis=0, tiled=True,
    ).reshape(all_tokens.shape[1], 3 * own)
    taps = lax.all_to_all(
        filter_taps.astype(jnp.bfloat16).reshape(row_count, seq_size, own).transpose(1, 0, 2).reshape(seq_size, -1, 128),
        "seq", split_axis=0, concat_axis=0, tiled=True,
    ).reshape(total, own)
    gain = lax.dynamic_slice_in_dim(skip_gain, seq_index * own, own)
    projected = jnp.dot(all_tokens, weight, preferred_element_type=jnp.float32).astype(jnp.bfloat16)
    values, in_gate, out_gate = (
        projected[:, j * own : (j + 1) * own].astype(jnp.float32) for j in range(3)
    )
    signal = in_gate * values
    spec = dot32(table, signal)
    resp = dot32(table, taps)
    spec_re, spec_im, resp_re, resp_im = spec[:total], spec[total:], resp[:total], resp[total:]
    prod = jnp.concatenate(
        [spec_re * resp_re - spec_im * resp_im, -(spec_re * resp_im + spec_im * resp_re)]
    )
    conv = dot32(back, prod)
    gated = (out_gate * (conv + gain[None, :] * signal)).astype(jnp.bfloat16)
    mine = lax.all_to_all(gated.reshape(seq_size, row_count * own // 128, 128), "seq", split_axis=0, concat_axis=0, tiled=True)
    whole = lax.all_gather(mine, "ch", axis=0, tiled=True)
    whole = whole.reshape(-1, row_count, own).transpose(1, 0, 2).reshape(row_count, -1)
    return jnp.dot(whole, out_weight, preferred_element_type=jnp.float32).astype(jnp.bfloat16)


def fused_kernel(
    tokens, weight_hbm, taps_hbm, gain_hbm, out_weight, table_hbm, back_hbm, out,
    weight, taps, gain,
    all_tokens, pack_w, recv_w, full_w, pack_f, recv_f, all_taps, table, back, mix_w,
    resp, signal, split, out_gate, prod, pack_g, recv_g, wide,
    local_sem, w_send, w_recv, f_send, f_recv, up_send, down_send, z_recv, y_send, y_recv,
    c_send, c_recv, x_send, x_recv, k_send, k_recv, g_send, g_recv, h_send, h_recv,
):
    f32, bf16 = jnp.float32, jnp.bfloat16
    me, ch = lax.axis_index("seq"), lax.axis_index("ch")
    z, y = me // 2, me % 2
    rows, depth = tokens.shape[0], tokens.shape[1]
    part = rows // 4
    total = rows * 8
    half = rows // 2
    w_rows, chans = weight.shape[1:]
    own = chans // 8

    def flip(value, bit):
        return value + bit - 2 * bit * (value // bit % 2)

    x_ch, c_ch, d_ch = flip(ch, 2), flip(ch, 1), flip(flip(ch, 2), 1)
    mates = (c_ch, x_ch, d_ch)

    first_loads = [
        pltpu.make_async_copy(weight_hbm, weight, local_sem.at[4]),
        pltpu.make_async_copy(taps_hbm, taps, local_sem.at[5]),
        pltpu.make_async_copy(gain_hbm, gain, local_sem.at[6]),
    ]
    for load in first_loads:
        load.start()
    barrier = pltpu.get_barrier_semaphore()
    for k in range(1, 8):
        pl.semaphore_signal(
            barrier, inc=1, device_id={"seq": (me + k) % 8, "ch": ch},
            device_id_type=pl.DeviceIdType.MESH,
        )
    for mate in mates:
        pl.semaphore_signal(
            barrier, inc=1, device_id={"seq": me, "ch": mate}, device_id_type=pl.DeviceIdType.MESH
        )

    own_rows = pl.ds(pl.multiple_of(me * rows, rows), rows)
    loads = [
        pltpu.make_async_copy(tokens, all_tokens.at[own_rows, :], local_sem.at[0]),
        pltpu.make_async_copy(table_hbm, table, local_sem.at[1]),
        pltpu.make_async_copy(back_hbm, back, local_sem.at[2]),
        pltpu.make_async_copy(out_weight, mix_w, local_sem.at[3]),
    ]

    for load in first_loads:
        load.wait()
    for p in range(8):
        lanes = slice(p * own, (p + 1) * own)
        pack_f[p] = jnp.concatenate([taps[:half, lanes], taps[half:, lanes]], axis=1).astype(bf16)
        pack_w[p, :w_rows] = jnp.concatenate([weight[0, :, lanes], weight[1, :, lanes]], axis=1)
        pack_w[p, w_rows:] = jnp.concatenate(
            [weight[2, : w_rows // 2, lanes], weight[2, w_rows // 2 :, lanes]], axis=1
        )

    pl.semaphore_wait(barrier, 10)

    def remote(source, target, send, recv, seq_id, ch_id):
        return pltpu.make_async_remote_copy(
            src_ref=source, dst_ref=target, send_sem=send, recv_sem=recv,
            device_id={"seq": seq_id, "ch": ch_id}, device_id_type=pl.DeviceIdType.MESH,
        )

    def piece(seq_id, quarter):
        start = pl.multiple_of(seq_id * rows + quarter * part, part)
        return all_tokens.at[pl.ds(start, part), :]

    mine = tokens.at[pl.ds(pl.multiple_of(ch * part, part), part), :]

    def guarded(condition, action):
        if condition is None:
            action()
        else:
            pl.when(condition)(action)

    sent = []

    def send(condition, copy):
        guarded(condition, lambda: copy().start())
        sent.append((condition, copy))

    def z_copy(source, zs, step):
        sems = up_send if step > 0 else down_send
        return lambda: remote(source(), piece(2 * zs + y, ch), sems.at[zs], z_recv.at[zs], me + 2 * step, ch)

    def y_copy(source, zs):
        return lambda: remote(source(), piece(2 * zs + y, ch), y_send.at[zs], y_recv.at[zs], flip(me, 1), ch)

    send(z < 3, z_copy(lambda: mine, z, 1))
    send(z > 0, z_copy(lambda: mine, z, -1))
    send(None, y_copy(lambda: mine, z))

    def w_copy(k):
        p = (me + k) % 8
        return lambda: remote(pack_w.at[p], recv_w.at[me], w_send.at[k], w_recv.at[me], p, ch)

    def f_copy(k):
        p = (me + k) % 8
        return lambda: remote(pack_f.at[p], recv_f.at[me], f_send.at[k], f_recv.at[me], p, ch)

    order = (1, 7, 2, 6, 3, 5, 4)
    for k in order:
        send(None, f_copy(k))
    pending = list(order)

    def more(count):
        for k in pending[:count]:
            send(None, w_copy(k))
        del pending[:count]

    more(1)
    for load in loads:
        load.start()
    recv_w[me] = pack_w[me]
    recv_f[me] = pack_f[me]

    def spread(condition, s):
        send(condition, lambda: remote(piece(s, ch), piece(s, ch), c_send.at[s], c_recv.at[s], me, c_ch))
        send(condition, lambda: remote(piece(s, ch), piece(s, ch), x_send.at[s], x_recv.at[s], me, x_ch))

    def from_z(condition, zs, step):
        s = 2 * zs + y
        guarded(condition, lambda: z_copy(lambda: piece(s, ch), zs, step)().wait_recv())
        onward = (z < 3) if step > 0 else (z > 0)
        send(jnp.logical_and(condition, onward), z_copy(lambda: piece(s, ch), zs, step))
        send(condition, y_copy(lambda: piece(s, ch), zs))
        spread(condition, s)

    def from_y(condition, zs):
        s = 2 * zs + 1 - y
        guarded(condition, lambda: remote(
            piece(s, ch), piece(s, ch), y_send.at[zs], y_recv.at[zs], flip(me, 1), ch).wait_recv())
        spread(condition, s)

    def from_x(condition, s):
        guarded(condition, lambda: remote(
            piece(s, x_ch), piece(s, x_ch), x_send.at[s], x_recv.at[s], me, x_ch).wait_recv())
        send(condition, lambda: remote(
            piece(s, x_ch), piece(s, x_ch), k_send.at[s], k_recv.at[s], me, c_ch))

    tiles = [functools.partial(taps_tile, i, table, all_taps, resp) for i in range(8)]
    from_y(None, z)
    more(1)
    arrived = [(None, 2 * z + 1 - y)]
    for d in range(1, 4):
        below, above = z >= d, z + d <= 3
        from_z(below, z - d, 1)
        from_z(above, z + d, -1)
        more(1)
        if d == 1:
            taps_arrive(me, ch, remote, recv_f, f_send, f_recv, all_taps, half, own)
            loads[1].wait()
        else:
            tiles.pop(0)()
        from_y(below, z - d)
        tiles.pop(0)()
        from_y(above, z + d)
        more(1)
        tiles.pop(0)()
        for condition, zs in ((below, z - d), (above, z + d)):
            arrived += [(condition, 2 * zs + y), (condition, 2 * zs + 1 - y)]
    while arrived:
        from_x(*arrived.pop(0))
    while tiles:
        tiles.pop(0)()

    for k in range(1, 8):
        s = (me + k) % 8
        remote(recv_w.at[s], recv_w.at[s], w_send.at[k], w_recv.at[s], s, ch).wait_recv()
    for s in range(8):
        base = s * w_rows
        full_w[base : base + w_rows, : 2 * own] = recv_w[s, :w_rows]
        full_w[base : base + w_rows // 2, 2 * own :] = recv_w[s, w_rows:][:, :own]
        full_w[base + w_rows // 2 : base + w_rows, 2 * own :] = recv_w[s, w_rows:][:, own:]

    for k in range(1, 8):
        s = (me + k) % 8
        remote(piece(s, c_ch), piece(s, c_ch), c_send.at[s], c_recv.at[s], me, c_ch).wait_recv()
        remote(piece(s, d_ch), piece(s, d_ch), k_send.at[s], k_recv.at[s], me, c_ch).wait_recv()
    loads[0].wait()

    @pl.loop(0, total // 256)
    def _(i):
        at = pl.ds(pl.multiple_of(i * 256, 256), 256)
        proj = jnp.dot(all_tokens[at, :], full_w[...], preferred_element_type=f32)
        proj = proj.astype(bf16).astype(f32)
        sig = proj[:, own : 2 * own] * proj[:, :own]
        signal[at, :] = sig
        out_gate[at, :] = proj[:, 2 * own :]
        high = sig.astype(bf16)
        split[at, :] = jnp.concatenate([high, (sig - high.astype(f32)).astype(bf16)], axis=1)

    @pl.loop(0, total // 256)
    def _(i):
        at = pl.ds(pl.multiple_of(i * 256, 256), 256)
        under = pl.ds(pl.multiple_of(total + i * 256, 256), 256)
        re = jnp.dot(table[at, :], split[...], preferred_element_type=f32)
        im = jnp.dot(table[under, :], split[...], preferred_element_type=f32)
        re, im = re[:, :own] + re[:, own:], im[:, :own] + im[:, own:]
        filt_re, filt_im = resp[at, :], resp[under, :]
        prod[at, :] = (re * filt_re - im * filt_im).astype(bf16)
        prod[under, :] = (re * filt_im + im * filt_re).astype(bf16)

    skip = jnp.zeros((1, own), f32)
    for p in range(8):
        skip = skip + jnp.where(me == p, gain[:, p * own : (p + 1) * own], 0.0)

    loads[2].wait()

    def g_copy(k):
        p = (me + k) % 8
        return lambda: remote(pack_g.at[p], recv_g.at[ch, me], g_send.at[k], g_recv.at[me], p, ch)

    for k in (4, 3, 5, 2, 6, 1, 7, 0):
        p = (me + k) % 8
        at = pl.ds(pl.multiple_of(p * rows, rows), rows)
        conv = jnp.dot(back[at, :], prod[...], preferred_element_type=f32)
        gated = (out_gate[at, :] * (conv + skip * signal[at, :])).astype(bf16)
        packed = jnp.concatenate([gated[:half], gated[half:]], axis=1)
        if k:
            pack_g[p] = packed
            send(None, g_copy(k))
        else:
            recv_g[ch, me] = packed

    def h_copy(j, s):
        return lambda: remote(recv_g.at[ch, s], recv_g.at[ch, s], h_send.at[j, s], h_recv.at[j, s], me, mates[j])

    for k in (0, 1, 7, 2, 6, 3, 5, 4):
        s = (me + k) % 8
        if k:
            remote(recv_g.at[ch, s], recv_g.at[ch, s], g_send.at[k], g_recv.at[s], s, ch).wait_recv()
        for j in (1, 0):
            send(None, h_copy(j, s))
    for k in (0, 1, 7, 2, 6, 3, 5, 4):
        s = (me + k) % 8
        remote(
            recv_g.at[x_ch, s], recv_g.at[x_ch, s], h_send.at[1, s], h_recv.at[1, s], me, x_ch
        ).wait_recv()
        send(None, lambda s=s: remote(
            recv_g.at[x_ch, s], recv_g.at[x_ch, s], h_send.at[2, s], h_recv.at[2, s], me, c_ch))
    loads[3].wait()
    for j in (0, 2):
        for s in range(8):
            remote(
                recv_g.at[mates[j], s], recv_g.at[mates[j], s], h_send.at[j, s], h_recv.at[j, s], me, mates[j]
            ).wait_recv()
    for c in range(4):
        for s in range(0, 8, 2):
            base = (c * 8 + s) * own
            a, b = recv_g[c, s], recv_g[c, s + 1]
            wide[:half, base : base + 2 * own] = jnp.concatenate([a[:, :own], b[:, :own]], axis=1)
            wide[half:, base : base + 2 * own] = jnp.concatenate([a[:, own:], b[:, own:]], axis=1)
    out[...] = jnp.dot(wide[...], mix_w[...], preferred_element_type=f32).astype(bf16)
    for condition, copy in sent:
        guarded(condition, lambda copy=copy: copy().wait_send())


def taps_arrive(me, ch, remote, recv_f, f_send, f_recv, all_taps, half, own):
    for k in range(1, 8):
        s = (me + k) % 8
        remote(recv_f.at[s], recv_f.at[s], f_send.at[k], f_recv.at[s], s, ch).wait_recv()
    for s in range(8):
        base = 2 * s * half
        all_taps[base : base + half, :] = recv_f[s][:, :own]
        all_taps[base + half : base + 2 * half, :] = recv_f[s][:, own:]


def taps_tile(i, table, all_taps, resp):
    at = slice(i * 256, i * 256 + 256)
    resp[at, :] = jnp.dot(table[at, :], all_taps[...], preferred_element_type=jnp.float32)


def per_device_fused(tokens, in_weight, filter_taps, skip_gain, out_weight):
    rows, depth = tokens.shape
    w_rows, _, chans = in_weight.shape
    own = chans // 8
    total = 8 * rows
    width = out_weight.shape[1]
    cos_table, sin_table = half_step_tables(total)
    table = jnp.asarray(np.concatenate([cos_table, sin_table]), jnp.bfloat16)
    back = jnp.asarray(np.concatenate([cos_table.T, sin_table.T], axis=1) / total, jnp.bfloat16)
    f32, bf16 = jnp.float32, jnp.bfloat16
    vmem, anywhere = pl.BlockSpec(memory_space=pltpu.VMEM), pl.BlockSpec(memory_space=pl.ANY)
    dma = pltpu.SemaphoreType.DMA
    return pl.pallas_call(
        fused_kernel,
        out_shape=jax.ShapeDtypeStruct((rows, width), bf16),
        in_specs=[anywhere] * 7,
        out_specs=vmem,
        scratch_shapes=[
            pltpu.VMEM((3, w_rows, chans), bf16),
            pltpu.VMEM((rows, chans), f32),
            pltpu.VMEM((1, chans), f32),
            pltpu.VMEM((total, depth), bf16),
            pltpu.VMEM((8, w_rows * 3 // 2, 2 * own), bf16),
            pltpu.VMEM((8, w_rows * 3 // 2, 2 * own), bf16),
            pltpu.VMEM((8 * w_rows, 3 * own), bf16),
            pltpu.VMEM((8, rows // 2, 2 * own), bf16),
            pltpu.VMEM((8, rows // 2, 2 * own), bf16),
            pltpu.VMEM((total, own), bf16),
            pltpu.VMEM((2 * total, total), bf16),
            pltpu.VMEM((total, 2 * total), bf16),
            pltpu.VMEM(out_weight.shape, bf16),
            pltpu.VMEM((2 * total, own), f32),
            pltpu.VMEM((total, own), f32),
            pltpu.VMEM((total, 2 * own), bf16),
            pltpu.VMEM((total, own), f32),
            pltpu.VMEM((2 * total, own), bf16),
            pltpu.VMEM((8, rows // 2, 2 * own), bf16),
            pltpu.VMEM((4, 8, rows // 2, 2 * own), bf16),
            pltpu.VMEM((rows, out_weight.shape[0]), bf16),
            dma((7,)), dma((8,)), dma((8,)), dma((8,)), dma((8,)),
            dma((4,)), dma((4,)), dma((4,)), dma((4,)), dma((4,)),
            dma((8,)), dma((8,)), dma((8,)), dma((8,)), dma((8,)), dma((8,)),
            dma((8,)), dma((8,)), dma((3, 8)), dma((3, 8)),
        ],
        compiler_params=pltpu.CompilerParams(
            collective_id=0, has_side_effects=True, vmem_limit_bytes=60 * 2**20
        ),
    )(
        tokens, in_weight.transpose(1, 0, 2), filter_taps, skip_gain[None, :],
        out_weight, table, back,
    )


def solution(mesh):
    in_specs = (P("seq", None), P("seq", None, "ch"), P("seq", "ch"), P("ch"), P(None, "ch"))
    out_specs = P("seq", "ch")

    def whole(tokens, in_weight, filter_taps, skip_gain, out_weight):
        fits = mesh.shape["seq"] == 8 and mesh.shape["ch"] == 4
        fits = fits and tokens.shape[0] == 1024 and filter_taps.shape[1] == 2048
        if fits:
            body = per_device_fused
        else:
            body = per_device if tokens.shape[0] <= DENSE_LIMIT else per_device_long
        return jax.shard_map(
            body, mesh=mesh, in_specs=in_specs, out_specs=out_specs, check_vma=False
        )(tokens, in_weight, filter_taps, skip_gain, out_weight)

    return whole
```
